32 devices in a mesh: tm: 8 (over z, core), head: 4 (over y, x).
Axes of the slice: x: 2, y: 2, z: 4, core: 2. Of those that a mesh axis runs over, the one named last changes fastest.
Arguments:
- queries: bfloat16 [4096, 768], P(('tm', 'head')), may hold values from -64 to 64
- keys: bfloat16 [4096, 768], P(('tm', 'head')), may hold values from -4 to 4
- values: bfloat16 [4096, 768], P(('tm', 'head')), may hold values from -6 to 6
- grad_out: bfloat16 [4096, 768], P(('tm', 'head')), may hold values from -6 to 6
- frame_counts: int32 [4], replicated, may hold values from 1 to 2048, 4096 in all
Outputs:
- attended: bfloat16 [4096, 768], P(('tm', 'head'))
- grad_queries: bfloat16 [4096, 768], P(('tm', 'head'))
- grad_keys: bfloat16 [4096, 768], P(('tm', 'head'))
- grad_values: bfloat16 [4096, 768], P(('tm', 'head'))
The draws below stay inside these ranges and needn't reach their ends.
All inputs are finite; a program needn't handle non-finite values.
Results may differ from the reference program's by a relative error of at most 0.029.
Values may be sent and summed in bfloat16 or wider, within the bound.
A program may use at most 64 MiB of HBM per device.

```python
import math
import jax
import jax.numpy as jnp
import numpy as np
from jax import lax

HEADS = 8
DH = 96
NUTT = 4
TOTAL = 4096
MOST = 2048


def paired_draw(key):
    base = jax.random.fold_in(key, 11)
    key_query, key_keys = jax.random.split(base, 2)
    shape = (TOTAL, HEADS * DH)
    query = jnp.clip(3.0 * jax.random.normal(key_query, shape, jnp.float32), -18.0, 18.0)
    keyset = jnp.clip(jax.random.normal(key_keys, shape, jnp.float32), -4.0, 4.0)
    return (query, keyset)


def draw_queries(key, part):
    return paired_draw(key)[0].astype(jnp.bfloat16)


def draw_keys(key, part):
    return paired_draw(key)[1].astype(jnp.bfloat16)


def shard_levels(own_key, extent, pieces, least, top_value):
    factor_of, own = 1.0, jax.random.fold_in(own_key, 6)
    for position, parts in pieces:
        steps = jnp.exp(jax.random.uniform(jax.random.fold_in(own, position), (parts,), jnp.float32, least / len(pieces), top_value / len(pieces)))
        factor_of = factor_of * jnp.repeat(steps, extent[position] // parts).reshape([-1 if axis == position else 1 for axis in range(len(extent))])
    return factor_of


def profile(count, total, limit, slope):
    weights = [(1 << 20) // math.isqrt(standing ** slope) + 1 for standing in range(2, count + 1)]
    spare, given = total - limit - (count - 1), [1] * (count - 1)
    while spare > 0:
        free = [i for i in range(count - 1) if given[i] < limit]
        mass, left = sum([weights[i] for i in free]), spare
        for i in free:
            extra = min(limit - given[i], max(1, left * weights[i] // mass), spare)
            given[i] = given[i] + extra
            spare = spare - extra
    return np.array([limit] + given)


def ragged(rng, amount, total, most, slope):
    if amount == 2:
        one = jax.random.randint(rng, (), max(1, total - most), min(most, total - 1) + 1)
        return jnp.stack([one, total - one])
    tallies = jnp.asarray(profile(amount, total, most, slope), jnp.int32)
    pairs = (amount - 1) // 2
    giver, sink = tallies[1:1 + 2 * pairs:2], tallies[2:2 + 2 * pairs:2]
    room = jnp.minimum(giver - 1, most - sink)
    moved = jax.random.randint(jax.random.fold_in(rng, 1), (pairs,), 0, 1 << 20) % (room + 1)
    tallies = tallies.at[1:1 + 2 * pairs:2].set(giver - moved).at[2:2 + 2 * pairs:2].set(sink + moved)
    return tallies[jax.random.permutation(jax.random.fold_in(rng, 2), amount)]


def normal_values(stream_key, shape, width, most, cuts=(), held_as=jnp.bfloat16):
    entries = width * jax.random.normal(stream_key, shape, jnp.float32)
    if cuts:
        entries = entries * shard_levels(stream_key, shape, cuts, -0.22, 0.18)
    return jnp.clip(entries, -most, most).astype(held_as)


def setup_inputs(seed: int = 0) -> dict:
    seeds = jax.random.split(jax.random.key(seed), 6)
    return {
        "queries": draw_queries(jax.random.fold_in(seeds[5], 71), 0),
        "keys": draw_keys(jax.random.fold_in(seeds[5], 71), 0),
        "values": normal_values(seeds[2], (TOTAL, HEADS * DH), 1.0, 6.0, ((0, 32),)),
        "grad_out": normal_values(seeds[3], (TOTAL, HEADS * DH), 1.0, 6.0, ((0, 32),)),
        "frame_counts": ragged(seeds[4], NUTT, TOTAL, MOST, 2).astype(jnp.int32),
    }


def segment_of(index, bounds):
    return lax.optimization_barrier(jnp.sum((index[:, None] >= bounds[None, :]).astype(jnp.int32), axis=1))

def reference(queries, keys, values, grad_out, frame_counts):
    scale = 1.0 / math.sqrt(DH)
    bounds = jnp.cumsum(frame_counts).astype(jnp.int32)[:NUTT - 1]
    seg_all = segment_of(jnp.arange(TOTAL, dtype=jnp.int32), bounds)
    block = math.gcd(TOTAL, 1024)
    nblocks = TOTAL // block

    def split_heads(array):
        return array.reshape(TOTAL, HEADS, DH).transpose(1, 0, 2)

    def one_head(arrays):
        query_h, key_h, value_h, grad_h = arrays

        def step(carry, index):
            acc_keys, acc_values = carry
            start = (index * block).astype(jnp.int32)
            query_blk = lax.dynamic_slice_in_dim(query_h, start, block, 0)
            grad_blk = lax.dynamic_slice_in_dim(grad_h, start, block, 0)
            seg_blk = lax.dynamic_slice_in_dim(seg_all, start, block, 0)
            visible = seg_blk[:, None] == seg_all[None, :]
            scores = jnp.dot(query_blk, key_h.T, preferred_element_type=jnp.float32) * scale
            top = lax.optimization_barrier(jnp.max(jnp.where(visible, scores, -1e+30), axis=1))
            forward_low = jnp.where(visible, jnp.exp(scores - top[:, None]), 0.0)
            total = lax.optimization_barrier(jnp.sum(forward_low, axis=1))
            log_total = top + jnp.log(total)
            forward_low = forward_low.astype(jnp.bfloat16)
            attended = (jnp.dot(forward_low, value_h, preferred_element_type=jnp.float32) / total[:, None]).astype(jnp.bfloat16)
            weights = jnp.where(visible, jnp.exp(scores - log_total[:, None]), 0.0)
            weights_low = weights.astype(jnp.bfloat16)
            delta = lax.optimization_barrier(jnp.sum(grad_blk.astype(jnp.float32) * attended.astype(jnp.float32), axis=1))
            dprod = jnp.dot(grad_blk, value_h.T, preferred_element_type=jnp.float32)
            dscore = (weights * (dprod - delta[:, None])).astype(jnp.bfloat16)
            grad_q = (scale * jnp.dot(dscore, key_h, preferred_element_type=jnp.float32)).astype(jnp.bfloat16)
            acc_keys = acc_keys + jnp.dot(dscore.T, query_blk, preferred_element_type=jnp.float32)
            acc_values = acc_values + jnp.dot(weights_low.T, grad_blk, preferred_element_type=jnp.float32)
            return ((acc_keys, acc_values), (attended, grad_q))
        zeros = jnp.zeros((TOTAL, DH), jnp.float32)
        (acc_keys, acc_values), (attended, grad_q) = lax.scan(step, (zeros, zeros), jnp.arange(nblocks, dtype=jnp.int32))
        return (attended.reshape(TOTAL, DH), grad_q.reshape(TOTAL, DH), (scale * acc_keys).astype(jnp.bfloat16), acc_values.astype(jnp.bfloat16))
    results = lax.map(one_head, (split_heads(queries), split_heads(keys), split_heads(values), split_heads(grad_out)))

    def join_heads(array):
        return array.transpose(1, 0, 2).reshape(TOTAL, HEADS * DH)
    return (join_heads(results[0]), join_heads(results[1]), join_heads(results[2]), join_heads(results[3]))
```

```python
import functools
import math

import jax
import jax.numpy as jnp
from jax import lax
from jax.experimental import pallas as pl
from jax.experimental.pallas import tpu as pltpu
from jax.sharding import PartitionSpec as P

HEADS = 8
DH = 96
MESH = pl.DeviceIdType.MESH
F32 = jnp.float32
BF16 = jnp.bfloat16


def greet(t, hd, T, H):
    barrier = pltpu.get_barrier_semaphore()
    for i in range(1, T):
        pl.semaphore_signal(barrier, inc=1, device_id=(lax.rem(t + i, T), hd), device_id_type=MESH)
    for j in range(1, H):
        pl.semaphore_signal(barrier, inc=1, device_id=(t, lax.rem(hd + j, H)), device_id_type=MESH)
    return barrier


def lanes(chunk, rows):
    return pl.ds(pl.multiple_of(chunk * rows, rows), rows)


def gather_kernel(T, H, R, q_ref, k_ref, v_ref, g_ref, kv, qg, kvs, qgs,
                  zs, zr, qs, qr, ps, pr):
    rows = q_ref.shape[0]
    t, hd = lax.axis_index("tm"), lax.axis_index("head")
    barrier = greet(t, hd, T, H)
    for n, (src, dst) in enumerate(((k_ref, kvs), (v_ref, kvs), (q_ref, qgs), (g_ref, qgs))):
        flat = src[...].T
        for h in range(HEADS):
            dst[h, n % 2] = flat[h * DH:(h + 1) * DH, :]
    pl.semaphore_wait(barrier, T + H - 2)

    def kv_copy(i, dest, owner):
        return pltpu.make_async_remote_copy(
            src_ref=kvs.at[lax.div(dest, R)], dst_ref=kv.at[:, :, lanes(owner * H + hd, rows)],
            send_sem=zs.at[i], recv_sem=zr.at[i], device_id=(dest, hd), device_id_type=MESH)

    def qg_copy(i, dest, owner):
        return pltpu.make_async_remote_copy(
            src_ref=qgs.at[lax.div(dest, R)], dst_ref=qg.at[:, :, lanes(lax.div(owner, R), rows)],
            send_sem=qs.at[i], recv_sem=qr.at[i], device_id=(dest, hd), device_id_type=MESH)

    def plane_copy(i, j, source, column):
        where = kv.at[:, :, lanes(source * H + column, rows)]
        return pltpu.make_async_remote_copy(
            src_ref=where, dst_ref=where, send_sem=ps.at[i, j], recv_sem=pr.at[i, j],
            device_id=(t, lax.rem(hd + j, H)), device_id_type=MESH)

    for i in range(1, T):
        kv_copy(i, lax.rem(t + i, T), t).start()
    for i in range(R, T, R):
        qg_copy(i, lax.rem(t + i, T), t).start()
    kv[:, :, lanes(t * H + hd, rows)] = kvs[lax.div(t, R)]
    qg[:, :, lanes(lax.div(t, R), rows)] = qgs[lax.div(t, R)]
    for i in range(T):
        source = lax.rem(t + T - i, T)
        if i:
            kv_copy(i, lax.rem(t + i, T), source).wait_recv()
        for j in range(1, H):
            plane_copy(i, j, source, hd).start()
    for i in range(T):
        source = lax.rem(t + T - i, T)
        for j in range(1, H):
            plane_copy(i, j, source, hd).wait_send()
            plane_copy(i, j, source, lax.rem(hd + H - j, H)).wait_recv()
        if i:
            kv_copy(i, lax.rem(t + i, T), t).wait_send()
        if i and i % R == 0:
            qg_copy(i, lax.rem(t + i, T), source).wait()


def scatter_kernel(T, H, R, oq, dkv, att, gq, gk, gv, part, summed, home_o, home_k,
                   ps, pr, os_, or_, ks, kr):
    rows = att.shape[0]
    t, hd = lax.axis_index("tm"), lax.axis_index("head")
    barrier = greet(t, hd, T, H)
    pl.semaphore_wait(barrier, T + H - 2)

    def plane_copy(i, j, target, column):
        return pltpu.make_async_remote_copy(
            src_ref=dkv.at[:, :, lanes(target * H + column, rows)], dst_ref=part.at[j - 1, target],
            send_sem=ps.at[i, j], recv_sem=pr.at[i, j], device_id=(t, column), device_id_type=MESH)

    def o_copy(i, dest, owner):
        return pltpu.make_async_remote_copy(
            src_ref=oq.at[:, :, lanes(lax.div(dest, R), rows)], dst_ref=home_o.at[lax.div(owner, R)],
            send_sem=os_.at[i], recv_sem=or_.at[i], device_id=(dest, hd), device_id_type=MESH)

    def k_copy(i, dest, owner):
        return pltpu.make_async_remote_copy(
            src_ref=summed.at[dest], dst_ref=home_k.at[owner],
            send_sem=ks.at[i], recv_sem=kr.at[i], device_id=(dest, hd), device_id_type=MESH)

    order = list(range(1, T)) + [0]
    for i in order:
        for j in range(1, H):
            plane_copy(i, j, lax.rem(t + i, T), lax.rem(hd + j, H)).start()
    for i in range(R, T, R):
        o_copy(i, lax.rem(t + i, T), t).start()
    home_o[lax.div(t, R)] = oq[:, :, lanes(lax.div(t, R), rows)]
    for i in order:
        target = lax.rem(t + i, T)
        total = dkv[:, :, lanes(target * H + hd, rows)].astype(F32)
        for j in range(1, H):
            plane_copy(i, j, target, lax.rem(hd + j, H)).wait_recv()
            total = total + part[j - 1, target].astype(F32)
        if i:
            summed[target] = total.astype(BF16)
            k_copy(i, target, t).start()
        else:
            home_k[t] = total.astype(BF16)
    for i in range(R, T, R):
        o_copy(i, lax.rem(t + i, T), lax.rem(t + T - i, T)).wait()
    att[...] = home_o[:, 0].reshape(HEADS * DH, rows).T
    gq[...] = home_o[:, 1].reshape(HEADS * DH, rows).T
    for i in order:
        target = lax.rem(t + i, T)
        for j in range(1, H):
            plane_copy(i, j, target, lax.rem(hd + j, H)).wait_send()
        if i:
            k_copy(i, target, lax.rem(t + T - i, T)).wait()
    for n, out in enumerate((gk, gv)):
        terms = home_k[:, n]
        if R > 1:
            terms = jnp.sum(terms.reshape(HEADS, R, DH, rows).astype(F32), axis=1).astype(BF16)
        out[...] = terms.reshape(HEADS * DH, rows).T


def attention_kernel(T, H, R, kblock, counts, kv, qg, oq, dkv, key, value, score, dkey, dvalue):
    total_rows = kv.shape[2]
    rows = total_rows // (T * H)
    wide = 2 * rows
    pairs = qg.shape[2] // wide
    scale = 1.0 / math.sqrt(DH)
    t, hd = lax.axis_index("tm"), lax.axis_index("head")
    bounds = []
    edge = 0
    for n in range(counts.shape[0]):
        edge = edge + counts[n]
        bounds.append(edge)
    bounds[-1] = total_rows

    def first(frame):
        low = jnp.zeros_like(frame)
        for bound in bounds[:-1]:
            low = jnp.where(frame >= bound, bound, low)
        return low

    def last(frame):
        high = jnp.zeros_like(frame) + total_rows
        for bound in bounds[-2::-1]:
            high = jnp.where(frame < bound, bound, high)
        return high

    @pl.loop(0, total_rows // rows)
    def _(c):
        at = pl.ds(pl.multiple_of(c * rows, rows), rows)
        key[at, :] = kv[0, :, at].T
        value[at, :] = kv[1, :, at].T
        dkey[at, :] = jnp.zeros((rows, DH), F32)
        dvalue[at, :] = jnp.zeros((rows, DH), F32)

    @pl.loop(0, pairs)
    def _(p):
        cols = pl.ds(pl.multiple_of(p * wide, wide), wide)
        qt, gt = qg[0, :, cols], qg[1, :, cols]
        q, g = qt.T, gt.T
        base0 = ((2 * p * R + lax.rem(t, R)) * H + hd) * rows
        base1 = (((2 * p + 1) * R + lax.rem(t, R)) * H + hd) * rows
        lane = lax.broadcasted_iota(jnp.int32, (1, wide), 1)
        frame = jnp.where(lane < rows, base0 + lane, base1 + lane - rows)
        low, high = first(frame), last(frame)
        begin = lax.div(first(base0), kblock)
        end = lax.div(last(base1 + rows - 1) + kblock - 1, kblock)

        def span(b):
            return pl.ds(pl.multiple_of(b * kblock, kblock), kblock)

        def scores(b, top):
            s = jnp.dot(key[span(b), :], qt, preferred_element_type=F32)
            s = s * (scale * math.log2(math.e))
            at = b * kblock + lax.broadcasted_iota(jnp.int32, (kblock, wide), 0)
            s = jnp.where((at >= low) & (at < high), s, -1e30)
            score[span(b), :] = s
            return jnp.maximum(top, jnp.max(s, axis=0, keepdims=True))

        top = lax.fori_loop(begin, end, scores, jnp.full((1, wide), -1e30, F32))

        def forward(b, carry):
            total, out = carry
            e = jnp.exp2(score[span(b), :] - top)
            score[span(b), :] = e
            out = out + jnp.dot(kv[1, :, span(b)], e.astype(BF16), preferred_element_type=F32)
            return total + jnp.sum(e, axis=0, keepdims=True), out

        total, out = lax.fori_loop(
            begin, end, forward, (jnp.zeros((1, wide), F32), jnp.zeros((DH, wide), F32)))
        attended = (out / total).astype(BF16)
        oq[0, :, cols] = attended
        delta = jnp.sum(gt.astype(F32) * attended.astype(F32), axis=0, keepdims=True)
        share = 1.0 / total

        def backward(b, dq):
            w = score[span(b), :] * share
            dprod = jnp.dot(value[span(b), :], gt, preferred_element_type=F32)
            ds = (w * (dprod - delta)).astype(BF16)
            dkey[span(b), :] += jnp.dot(ds, q, preferred_element_type=F32)
            dvalue[span(b), :] += jnp.dot(w.astype(BF16), g, preferred_element_type=F32)
            return dq + jnp.dot(kv[0, :, span(b)], ds, preferred_element_type=F32)

        dq = lax.fori_loop(begin, end, backward, jnp.zeros((DH, wide), F32))
        oq[1, :, cols] = (dq * scale).astype(BF16)

    @pl.loop(0, total_rows // rows)
    def _(c):
        at = pl.ds(pl.multiple_of(c * rows, rows), rows)
        dkv[0, :, at] = (dkey[at, :] * scale).T.astype(BF16)
        dkv[1, :, at] = dvalue[at, :].T.astype(BF16)


def body(queries, keys, values, grad_out, frame_counts):
    T, H = lax.axis_size("tm"), lax.axis_size("head")
    R = T // HEADS
    rows = queries.shape[0]
    total_rows = rows * T * H
    mine = HEADS * rows
    vmem = pl.BlockSpec(memory_space=pltpu.VMEM)
    smem = pl.BlockSpec(memory_space=pltpu.SMEM)
    dma = pltpu.SemaphoreType.DMA
    kv, qg = pl.pallas_call(
        functools.partial(gather_kernel, T, H, R),
        out_shape=(jax.ShapeDtypeStruct((2, DH, total_rows), BF16),
                   jax.ShapeDtypeStruct((2, DH, mine), BF16)),
        in_specs=[vmem] * 4,
        out_specs=(vmem, vmem),
        scratch_shapes=[
            pltpu.VMEM((HEADS, 2, DH, rows), BF16), pltpu.VMEM((HEADS, 2, DH, rows), BF16),
            dma((T,)), dma((T,)), dma((T,)), dma((T,)), dma((T, H)), dma((T, H))],
        compiler_params=pltpu.CompilerParams(
            collective_id=0, has_side_effects=True, vmem_limit_bytes=48 << 20),
        name="gather",
    )(queries, keys, values, grad_out)
    oq, dkv = pl.pallas_call(
        functools.partial(attention_kernel, T, H, R, 512),
        out_shape=(jax.ShapeDtypeStruct((2, DH, mine), BF16),
                   jax.ShapeDtypeStruct((2, DH, total_rows), BF16)),
        in_specs=[smem, vmem, vmem],
        out_specs=(vmem, vmem),
        scratch_shapes=[
            pltpu.VMEM((total_rows, DH), BF16), pltpu.VMEM((total_rows, DH), BF16),
            pltpu.VMEM((total_rows, 2 * rows), F32),
            pltpu.VMEM((total_rows, DH), F32), pltpu.VMEM((total_rows, DH), F32)],
        compiler_params=pltpu.CompilerParams(vmem_limit_bytes=60 << 20),
        name="attention",
    )(frame_counts, kv, qg)
    block = jax.ShapeDtypeStruct((rows, HEADS * DH), BF16)
    return pl.pallas_call(
        functools.partial(scatter_kernel, T, H, R),
        out_shape=(block,) * 4,
        in_specs=[vmem, vmem],
        out_specs=(vmem,) * 4,
        scratch_shapes=[
            pltpu.VMEM((H - 1, T, 2, DH, rows), BF16), pltpu.VMEM((T, 2, DH, rows), BF16),
            pltpu.VMEM((HEADS, 2, DH, rows), BF16), pltpu.VMEM((T, 2, DH, rows), BF16),
            dma((T, H)), dma((T, H)), dma((T,)), dma((T,)), dma((T,)), dma((T,))],
        compiler_params=pltpu.CompilerParams(
            collective_id=1, has_side_effects=True, vmem_limit_bytes=48 << 20),
        name="scatter",
    )(oq, dkv)


def solution(mesh):
    split = P(("tm", "head"), None)
    return jax.shard_map(
        body, mesh=mesh, in_specs=(split,) * 4 + (P(),), out_specs=(split,) * 4, check_vma=False)
```

```python
import functools
import math

import jax
import jax.numpy as jnp
from jax import lax
from jax.experimental import pallas as pl
from jax.experimental.pallas import tpu as pltpu
from jax.sharding import PartitionSpec as P

HEADS = 8
DH = 96
LANES = 128
MESH = pl.DeviceIdType.MESH
F32 = jnp.float32
BF16 = jnp.bfloat16


def greet(t, hd, T, H):
    barrier = pltpu.get_barrier_semaphore()
    for i in range(1, T):
        pl.semaphore_signal(barrier, inc=1, device_id=(lax.rem(t + i, T), hd), device_id_type=MESH)
    for j in range(1, H):
        pl.semaphore_signal(barrier, inc=1, device_id=(t, lax.rem(hd + j, H)), device_id_type=MESH)
    return barrier


def lanes(chunk, rows):
    return pl.ds(pl.multiple_of(chunk * rows, rows), rows)


def gather_kernel(T, H, R, q_ref, k_ref, v_ref, g_ref, kv, qg, kvs, qgs, held,
                  ls, zs, zr, qs, qr, ps, pr):
    rows = q_ref.shape[0]
    loads = [pltpu.make_async_copy(ref, held.at[n], ls.at[n])
             for n, ref in enumerate((k_ref, v_ref, q_ref, g_ref))]
    for load in loads:
        load.start()
    t, hd = lax.axis_index("tm"), lax.axis_index("head")
    barrier = greet(t, hd, T, H)
    for n, dst in enumerate((kvs, kvs, qgs, qgs)):
        loads[n].wait()
        flat = held[n].T
        for h in range(HEADS):
            dst[h, n % 2] = flat[h * DH:(h + 1) * DH, :]
    pl.semaphore_wait(barrier, T + H - 2)

    def kv_copy(i, dest, owner):
        return pltpu.make_async_remote_copy(
            src_ref=kvs.at[lax.div(dest, R)], dst_ref=kv.at[:, :, lanes(owner * H + hd, rows)],
            send_sem=zs.at[i], recv_sem=zr.at[i], device_id=(dest, hd), device_id_type=MESH)

    def qg_copy(i, dest, owner):
        return pltpu.make_async_remote_copy(
            src_ref=qgs.at[lax.div(dest, R)], dst_ref=qg.at[:, :, lanes(lax.div(owner, R), rows)],
            send_sem=qs.at[i], recv_sem=qr.at[i], device_id=(dest, hd), device_id_type=MESH)

    def plane_copy(i, j, source, column):
        where = kv.at[:, :, lanes(source * H + column, rows)]
        return pltpu.make_async_remote_copy(
            src_ref=where, dst_ref=where, send_sem=ps.at[i, j], recv_sem=pr.at[i, j],
            device_id=(t, lax.rem(hd + j, H)), device_id_type=MESH)

    for i in range(1, T):
        kv_copy(i, lax.rem(t + i, T), t).start()
    for i in range(R, T, R):
        qg_copy(i, lax.rem(t + i, T), t).start()
    kv[:, :, lanes(t * H + hd, rows)] = kvs[lax.div(t, R)]
    qg[:, :, lanes(lax.div(t, R), rows)] = qgs[lax.div(t, R)]
    for i in range(T):
        source = lax.rem(t + T - i, T)
        if i:
            kv_copy(i, lax.rem(t + i, T), source).wait_recv()
        for j in range(1, H):
            plane_copy(i, j, source, hd).start()
    for i in range(T):
        source = lax.rem(t + T - i, T)
        for j in range(1, H):
            plane_copy(i, j, source, hd).wait_send()
            plane_copy(i, j, source, lax.rem(hd + H - j, H)).wait_recv()
        if i:
            kv_copy(i, lax.rem(t + i, T), t).wait_send()
        if i and i % R == 0:
            qg_copy(i, lax.rem(t + i, T), source).wait()


def scatter_kernel(T, H, R, oq, dkv, att, gq, gk, gv, part, own, summed, home_o, home_k,
                   ls, ps, pr, os_, or_, ks, kr):
    rows = att.shape[0]
    t, hd = lax.axis_index("tm"), lax.axis_index("head")
    barrier = greet(t, hd, T, H)

    def own_load(i):
        target = lax.rem(t + i, T)
        return pltpu.make_async_copy(
            dkv.at[:, :, lanes(target * H + hd, rows)], own.at[target], ls.at[i])

    own_out = pltpu.make_async_copy(
        oq.at[:, :, lanes(lax.div(t, R), rows)], home_o.at[lax.div(t, R)], ls.at[T])
    for i in range(T):
        own_load(i).start()
    own_out.start()
    pl.semaphore_wait(barrier, T + H - 2)

    def plane_copy(i, j, target, column):
        return pltpu.make_async_remote_copy(
            src_ref=dkv.at[:, :, lanes(target * H + column, rows)], dst_ref=part.at[j - 1, target],
            send_sem=ps.at[i, j], recv_sem=pr.at[i, j], device_id=(t, column), device_id_type=MESH)

    def o_copy(i, dest, owner):
        return pltpu.make_async_remote_copy(
            src_ref=oq.at[:, :, lanes(lax.div(dest, R), rows)], dst_ref=home_o.at[lax.div(owner, R)],
            send_sem=os_.at[i], recv_sem=or_.at[i], device_id=(dest, hd), device_id_type=MESH)

    def k_copy(i, dest, owner):
        return pltpu.make_async_remote_copy(
            src_ref=summed.at[dest], dst_ref=home_k.at[owner],
            send_sem=ks.at[i], recv_sem=kr.at[i], device_id=(dest, hd), device_id_type=MESH)

    order = list(range(1, T)) + [0]
    for i in order:
        for j in range(1, H):
            plane_copy(i, j, lax.rem(t + i, T), lax.rem(hd + j, H)).start()
    for i in range(R, T, R):
        o_copy(i, lax.rem(t + i, T), t).start()
    for i in order:
        target = lax.rem(t + i, T)
        own_load(i).wait()
        total = own[target].astype(F32)
        for j in range(1, H):
            plane_copy(i, j, target, lax.rem(hd + j, H)).wait_recv()
            total = total + part[j - 1, target].astype(F32)
        if i:
            summed[target] = total.astype(BF16)
            k_copy(i, target, t).start()
        else:
            home_k[t] = total.astype(BF16)
    for i in range(R, T, R):
        o_copy(i, lax.rem(t + i, T), lax.rem(t + T - i, T)).wait()
    own_out.wait()
    att[...] = home_o[:, 0].reshape(HEADS * DH, rows).T
    gq[...] = home_o[:, 1].reshape(HEADS * DH, rows).T
    for i in order:
        target = lax.rem(t + i, T)
        for j in range(1, H):
            plane_copy(i, j, target, lax.rem(hd + j, H)).wait_send()
        if i:
            k_copy(i, target, lax.rem(t + T - i, T)).wait()
    for n, out in enumerate((gk, gv)):
        terms = home_k[:, n]
        if R > 1:
            terms = jnp.sum(terms.reshape(HEADS, R, DH, rows).astype(F32), axis=1).astype(BF16)
        out[...] = terms.reshape(HEADS * DH, rows).T


def attention_kernel(T, H, R, kblock, counts, kv, qg, oq, dkv, key, value, score, peak, dkey, dvalue):
    total_rows = kv.shape[2]
    rows = total_rows // (T * H)
    wide = 2 * rows
    pairs = qg.shape[2] // wide
    spare = key.shape[1] - DH
    scale = 1.0 / math.sqrt(DH)
    power = scale * math.log2(math.e)
    dkey[...] = jnp.zeros_like(dkey)
    dvalue[...] = jnp.zeros_like(dvalue)
    t, hd = lax.axis_index("tm"), lax.axis_index("head")
    bounds = []
    edge = 0
    for n in range(counts.shape[0] - 1):
        edge = edge + counts[n]
        bounds.append(edge)

    def first(frame):
        low = jnp.int32(0)
        for bound in bounds:
            low = jnp.where(frame >= bound, bound, low)
        return low

    def last(frame):
        high = jnp.int32(total_rows)
        for bound in bounds[::-1]:
            high = jnp.where(frame < bound, bound, high)
        return high

    def utterance(frame):
        index = jnp.zeros_like(frame)
        for bound in bounds:
            index = index + (frame >= bound).astype(jnp.int32)
        return index

    def line(n):
        return lax.broadcasted_iota(jnp.int32, (spare, n), 0)

    @pl.loop(0, total_rows // rows, unroll=8)
    def _(c):
        at = pl.ds(pl.multiple_of(c * rows, rows), rows)
        frame = c * rows + lax.broadcasted_iota(jnp.int32, (1, rows), 1)
        member = jnp.where(line(rows) == utterance(frame), 1.0, 0.0).astype(BF16)
        ones = jnp.where(line(rows) < 3, 1.0, 0.0).astype(BF16)
        key[at, :] = jnp.concatenate([kv[0, :, at], member], axis=0).T
        value[at, :] = jnp.concatenate([kv[1, :, at], ones], axis=0).T

    @pl.loop(0, pairs)
    def _(p):
        cols = pl.ds(pl.multiple_of(p * wide, wide), wide)
        qt, gt = qg[0, :, cols], qg[1, :, cols]
        q, g = qt.T, gt.T
        base0 = ((2 * p * R + lax.rem(t, R)) * H + hd) * rows
        base1 = (((2 * p + 1) * R + lax.rem(t, R)) * H + hd) * rows
        lane = lax.broadcasted_iota(jnp.int32, (1, wide), 1)
        frame = jnp.where(lane < rows, base0 + lane, base1 + lane - rows)
        hidden = (line(wide) != utterance(frame)) & (line(wide) < counts.shape[0])
        qt = jnp.concatenate([qt, jnp.where(hidden, -1e30, 0.0).astype(BF16)], axis=0)
        begin = lax.div(first(base0), kblock)
        end = lax.div(last(base1 + rows - 1) + kblock - 1, kblock)

        def span(b):
            return pl.ds(pl.multiple_of(b * kblock, kblock), kblock)

        def fold(x, op):
            parts = [x[n * 64:(n + 1) * 64] for n in range(kblock // 64)]
            while len(parts) > 1:
                parts = [op(parts[2 * n], parts[2 * n + 1]) for n in range(len(parts) // 2)]
            return parts[0]

        def forward(b, carry):
            reach, total, out = carry
            s = jnp.dot(key[span(b), :], qt, preferred_element_type=F32)
            top = jnp.maximum(reach, jnp.max(fold(s, jnp.maximum), axis=0, keepdims=True))
            e = jnp.exp2((s - top) * power)
            fade = jnp.exp2((reach - top) * power)
            score[span(b), :] = e
            peak[pl.ds(b, 1), :] = top
            out = out * fade + jnp.dot(kv[1, :, span(b)], e.astype(BF16), preferred_element_type=F32)
            return top, total * fade + jnp.sum(fold(e, jnp.add), axis=0, keepdims=True), out

        top, total, out = lax.fori_loop(
            begin, end, forward, (jnp.full((1, wide), -1e30, F32), jnp.zeros((1, wide), F32), jnp.zeros((DH, wide), F32)))
        attended = (out / total).astype(BF16)
        oq[0, :, cols] = attended
        delta = jnp.sum(gt.astype(F32) * attended.astype(F32), axis=0, keepdims=True)
        share = 1.0 / total
        tail, left = jnp.zeros((spare, wide), F32), -delta
        for n in range(3):
            piece = left.astype(BF16).astype(F32)
            tail = jnp.where(line(wide) == n, piece, tail)
            left = left - piece
        gt = jnp.concatenate([gt, tail.astype(BF16)], axis=0)

        def backward(b, dq):
            w = score[span(b), :] * (share * jnp.exp2((peak[pl.ds(b, 1), :] - top) * power))
            ds = (w * jnp.dot(value[span(b), :], gt, preferred_element_type=F32)).astype(BF16)
            dkey[span(b), :] += jnp.dot(ds, q, preferred_element_type=F32)
            dvalue[span(b), :] += jnp.dot(w.astype(BF16), g, preferred_element_type=F32)
            return dq + jnp.dot(kv[0, :, span(b)], ds, preferred_element_type=F32)

        dq = lax.fori_loop(begin, end, backward, jnp.zeros((DH, wide), F32))
        oq[1, :, cols] = (dq * scale).astype(BF16)

    @pl.loop(0, total_rows // rows, unroll=8)
    def _(c):
        at = pl.ds(pl.multiple_of(c * rows, rows), rows)
        dkv[0, :, at] = (dkey[at, :] * scale).astype(BF16).T
        dkv[1, :, at] = dvalue[at, :].astype(BF16).T


def body(queries, keys, values, grad_out, frame_counts):
    T, H = lax.axis_size("tm"), lax.axis_size("head")
    R = T // HEADS
    rows = queries.shape[0]
    total_rows = rows * T * H
    mine = HEADS * rows
    kblock = 1024
    vmem = pl.BlockSpec(memory_space=pltpu.VMEM)
    hbm = pl.BlockSpec(memory_space=pltpu.HBM)
    place = pl.BlockSpec(memory_space=pl.ANY)
    smem = pl.BlockSpec(memory_space=pltpu.SMEM)
    dma = pltpu.SemaphoreType.DMA
    kv, qg = pl.pallas_call(
        functools.partial(gather_kernel, T, H, R),
        out_shape=(jax.ShapeDtypeStruct((2, DH, total_rows), BF16),
                   jax.ShapeDtypeStruct((2, DH, mine), BF16)),
        in_specs=[hbm] * 4,
        out_specs=(vmem, vmem),
        scratch_shapes=[
            pltpu.VMEM((HEADS, 2, DH, rows), BF16), pltpu.VMEM((HEADS, 2, DH, rows), BF16),
            pltpu.VMEM((4, rows, HEADS * DH), BF16), dma((4,)),
            dma((T,)), dma((T,)), dma((T,)), dma((T,)), dma((T, H)), dma((T, H))],
        compiler_params=pltpu.CompilerParams(
            collective_id=0, has_side_effects=True, vmem_limit_bytes=24 << 20),
        name="gather",
    )(queries, keys, values, grad_out)
    oq, dkv = pl.pallas_call(
        functools.partial(attention_kernel, T, H, R, kblock),
        out_shape=(jax.ShapeDtypeStruct((2, DH, mine), BF16),
                   jax.ShapeDtypeStruct((2, DH, total_rows), BF16)),
        in_specs=[smem, vmem, vmem],
        out_specs=(vmem, vmem),
        scratch_shapes=[
            pltpu.VMEM((total_rows, LANES), BF16), pltpu.VMEM((total_rows, LANES), BF16),
            pltpu.VMEM((total_rows, 2 * rows), F32),
            pltpu.VMEM((total_rows // kblock, 2 * rows), F32),
            pltpu.VMEM((total_rows, DH), F32), pltpu.VMEM((total_rows, DH), F32),
        ],
        compiler_params=pltpu.CompilerParams(vmem_limit_bytes=min(60 << 20, (8 << 20) + total_rows * 3584)),
        name="attention",
    )(frame_counts, kv, qg)
    block = jax.ShapeDtypeStruct((rows, HEADS * DH), BF16)
    return pl.pallas_call(
        functools.partial(scatter_kernel, T, H, R),
        out_shape=(block,) * 4,
        in_specs=[place, place],
        out_specs=(vmem,) * 4,
        scratch_shapes=[
            pltpu.VMEM((H - 1, T, 2, DH, rows), BF16),
            pltpu.VMEM((T, 2, DH, rows), BF16), pltpu.VMEM((T, 2, DH, rows), BF16),
            pltpu.VMEM((HEADS, 2, DH, rows), BF16), pltpu.VMEM((T, 2, DH, rows), BF16),
            dma((T + 1,)), dma((T, H)), dma((T, H)), dma((T,)), dma((T,)), dma((T,)), dma((T,))],
        compiler_params=pltpu.CompilerParams(
            collective_id=1, has_side_effects=True, vmem_limit_bytes=24 << 20),
        name="scatter",
    )(oq, dkv)


def solution(mesh):
    split = P(("tm", "head"), None)
    return jax.shard_map(
        body, mesh=mesh, in_specs=(split,) * 4 + (P(),), out_specs=(split,) * 4, check_vma=False)
```

```python
import functools
import math

import jax
import jax.numpy as jnp
from jax import lax
from jax.experimental import pallas as pl
from jax.experimental.pallas import tpu as pltpu
from jax.sharding import PartitionSpec as P

HEADS = 8
DH = 96
LANES = 128
MESH = pl.DeviceIdType.MESH
F32 = jnp.float32
BF16 = jnp.bfloat16


def greet(t, hd, T, H):
    barrier = pltpu.get_barrier_semaphore()
    for i in range(1, T):
        pl.semaphore_signal(barrier, inc=1, device_id=(lax.rem(t + i, T), hd), device_id_type=MESH)
    for j in range(1, H):
        pl.semaphore_signal(barrier, inc=1, device_id=(t, lax.rem(hd + j, H)), device_id_type=MESH)
    return barrier


def lanes(chunk, rows):
    return pl.ds(pl.multiple_of(chunk * rows, rows), rows)


def gather_kernel(T, H, R, q_ref, k_ref, v_ref, g_ref, kv, qg, kvs, qgs, held,
                  ls, zs, zr, qs, qr, ps, pr):
    rows = q_ref.shape[0]
    loads = [pltpu.make_async_copy(ref, held.at[n], ls.at[n])
             for n, ref in enumerate((k_ref, v_ref, q_ref, g_ref))]
    for load in loads:
        load.start()
    t, hd = lax.axis_index("tm"), lax.axis_index("head")
    barrier = greet(t, hd, T, H)

    def turn(dst, first):
        for n in range(2):
            loads[first + n].wait()
            flat = held[first + n].T
            for h in range(HEADS):
                dst[h, n] = flat[h * DH:(h + 1) * DH, :]

    turn(kvs, 0)
    pl.semaphore_wait(barrier, T + H - 2)

    def kv_copy(i, dest, owner):
        return pltpu.make_async_remote_copy(
            src_ref=kvs.at[lax.div(dest, R)], dst_ref=kv.at[:, :, lanes(owner * H + hd, rows)],
            send_sem=zs.at[i], recv_sem=zr.at[i], device_id=(dest, hd), device_id_type=MESH)

    def qg_copy(i, dest, owner):
        return pltpu.make_async_remote_copy(
            src_ref=qgs.at[lax.div(dest, R)], dst_ref=qg.at[:, :, lanes(lax.div(owner, R), rows)],
            send_sem=qs.at[i], recv_sem=qr.at[i], device_id=(dest, hd), device_id_type=MESH)

    def plane_copy(i, j, source, column):
        where = kv.at[:, :, lanes(source * H + column, rows)]
        return pltpu.make_async_remote_copy(
            src_ref=where, dst_ref=where, send_sem=ps.at[i, j], recv_sem=pr.at[i, j],
            device_id=(t, lax.rem(hd + j, H)), device_id_type=MESH)

    for i in range(1, T):
        kv_copy(i, lax.rem(t + i, T), t).start()
    kv[:, :, lanes(t * H + hd, rows)] = kvs[lax.div(t, R)]
    for j in range(1, H):
        plane_copy(0, j, t, hd).start()
    turn(qgs, 2)
    for i in range(R, T, R):
        qg_copy(i, lax.rem(t + i, T), t).start()
    qg[:, :, lanes(lax.div(t, R), rows)] = qgs[lax.div(t, R)]
    for i in range(1, T):
        source = lax.rem(t + T - i, T)
        kv_copy(i, lax.rem(t + i, T), source).wait_recv()
        for j in range(1, H):
            plane_copy(i, j, source, hd).start()
    for i in range(T):
        source = lax.rem(t + T - i, T)
        for j in range(1, H):
            plane_copy(i, j, source, hd).wait_send()
            plane_copy(i, j, source, lax.rem(hd + H - j, H)).wait_recv()
        if i:
            kv_copy(i, lax.rem(t + i, T), t).wait_send()
        if i and i % R == 0:
            qg_copy(i, lax.rem(t + i, T), source).wait()


def scatter_kernel(T, H, R, oq, dkv, att, gq, gk, gv, part, own, summed, home_o, home_k,
                   ls, ps, pr, os_, or_, ks, kr):
    rows = att.shape[0]
    t, hd = lax.axis_index("tm"), lax.axis_index("head")
    barrier = greet(t, hd, T, H)

    def own_load(i):
        target = lax.rem(t + i, T)
        return pltpu.make_async_copy(
            dkv.at[:, :, lanes(target * H + hd, rows)], own.at[target], ls.at[i])

    own_out = pltpu.make_async_copy(
        oq.at[:, :, lanes(lax.div(t, R), rows)], home_o.at[lax.div(t, R)], ls.at[T])
    for i in range(T):
        own_load(i).start()
    own_out.start()
    pl.semaphore_wait(barrier, T + H - 2)

    def plane_copy(i, j, target, column):
        return pltpu.make_async_remote_copy(
            src_ref=dkv.at[:, :, lanes(target * H + column, rows)], dst_ref=part.at[j - 1, target],
            send_sem=ps.at[i, j], recv_sem=pr.at[i, j], device_id=(t, column), device_id_type=MESH)

    def o_copy(i, dest, owner):
        return pltpu.make_async_remote_copy(
            src_ref=oq.at[:, :, lanes(lax.div(dest, R), rows)], dst_ref=home_o.at[lax.div(owner, R)],
            send_sem=os_.at[i], recv_sem=or_.at[i], device_id=(dest, hd), device_id_type=MESH)

    def k_copy(i, dest, owner):
        return pltpu.make_async_remote_copy(
            src_ref=summed.at[dest], dst_ref=home_k.at[owner],
            send_sem=ks.at[i], recv_sem=kr.at[i], device_id=(dest, hd), device_id_type=MESH)

    order = list(range(1, T)) + [0]
    for i in order:
        for j in range(1, H):
            plane_copy(i, j, lax.rem(t + i, T), lax.rem(hd + j, H)).start()
    for i in range(R, T, R):
        o_copy(i, lax.rem(t + i, T), t).start()
    for i in order:
        target = lax.rem(t + i, T)
        own_load(i).wait()
        total = own[target].astype(F32)
        for j in range(1, H):
            plane_copy(i, j, target, lax.rem(hd + j, H)).wait_recv()
            total = total + part[j - 1, target].astype(F32)
        if i:
            summed[target] = total.astype(BF16)
            k_copy(i, target, t).start()
        else:
            home_k[t] = total.astype(BF16)
    for i in range(R, T, R):
        o_copy(i, lax.rem(t + i, T), lax.rem(t + T - i, T)).wait()
    own_out.wait()
    att[...] = home_o[:, 0].reshape(HEADS * DH, rows).T
    gq[...] = home_o[:, 1].reshape(HEADS * DH, rows).T
    for i in order:
        target = lax.rem(t + i, T)
        for j in range(1, H):
            plane_copy(i, j, target, lax.rem(hd + j, H)).wait_send()
        if i:
            k_copy(i, target, lax.rem(t + T - i, T)).wait()
    for n, out in enumerate((gk, gv)):
        terms = home_k[:, n]
        if R > 1:
            terms = jnp.sum(terms.reshape(HEADS, R, DH, rows).astype(F32), axis=1).astype(BF16)
        out[...] = terms.reshape(HEADS * DH, rows).T


def attention_kernel(T, H, R, kblock, counts, kv, qg, oq, dkv, key, value, score, peak, dkey, dvalue):
    total_rows = kv.shape[2]
    rows = total_rows // (T * H)
    wide = 2 * rows
    pairs = qg.shape[2] // wide
    spare = key.shape[1] - DH
    scale = 1.0 / math.sqrt(DH)
    power = scale * math.log2(math.e)
    dkey[...] = jnp.zeros_like(dkey)
    dvalue[...] = jnp.zeros_like(dvalue)
    t, hd = lax.axis_index("tm"), lax.axis_index("head")
    bounds = []
    edge = 0
    for n in range(counts.shape[0] - 1):
        edge = edge + counts[n]
        bounds.append(edge)

    def first(frame):
        low = jnp.int32(0)
        for bound in bounds:
            low = jnp.where(frame >= bound, bound, low)
        return low

    def last(frame):
        high = jnp.int32(total_rows)
        for bound in bounds[::-1]:
            high = jnp.where(frame < bound, bound, high)
        return high

    def utterance(frame):
        index = jnp.zeros_like(frame)
        for bound in bounds:
            index = index + (frame >= bound).astype(jnp.int32)
        return index

    def line(n):
        return lax.broadcasted_iota(jnp.int32, (spare, n), 0)

    @pl.loop(0, total_rows // rows, unroll=8)
    def _(c):
        at = pl.ds(pl.multiple_of(c * rows, rows), rows)
        frame = c * rows + lax.broadcasted_iota(jnp.int32, (1, rows), 1)
        member = jnp.where(line(rows) == utterance(frame), 1.0, 0.0).astype(BF16)
        ones = jnp.where(line(rows) < 3, 1.0, 0.0).astype(BF16)
        key[at, :] = jnp.concatenate([kv[0, :, at], member], axis=0).T
        value[at, :] = jnp.concatenate([kv[1, :, at], ones], axis=0).T

    @pl.loop(0, pairs)
    def _(p):
        cols = pl.ds(pl.multiple_of(p * wide, wide), wide)
        qt, gt = qg[0, :, cols], qg[1, :, cols]
        q, g = qt.T, gt.T
        base0 = ((2 * p * R + lax.rem(t, R)) * H + hd) * rows
        base1 = (((2 * p + 1) * R + lax.rem(t, R)) * H + hd) * rows
        lane = lax.broadcasted_iota(jnp.int32, (1, wide), 1)
        frame = jnp.where(lane < rows, base0 + lane, base1 + lane - rows)
        hidden = (line(wide) != utterance(frame)) & (line(wide) < counts.shape[0])
        qt = jnp.concatenate([qt, jnp.where(hidden, -1e30, 0.0).astype(BF16)], axis=0)
        begin = lax.div(first(base0), kblock)
        end = lax.div(last(base1 + rows - 1) + kblock - 1, kblock)

        def span(b):
            return pl.ds(pl.multiple_of(b * kblock, kblock), kblock)

        def fold(x, op):
            parts = [x[n * 64:(n + 1) * 64] for n in range(kblock // 64)]
            while len(parts) > 1:
                parts = [op(parts[2 * n], parts[2 * n + 1]) for n in range(len(parts) // 2)]
            return parts[0]

        def forward(b, carry):
            reach, total, out = carry
            s = jnp.dot(key[span(b), :], qt, preferred_element_type=F32)
            top = jnp.maximum(reach, jnp.max(fold(s, jnp.maximum), axis=0, keepdims=True))
            e = jnp.exp2((s - top) * power)
            fade = jnp.exp2((reach - top) * power)
            score[span(b), :] = e
            peak[pl.ds(b, 1), :] = top
            out = out * fade + jnp.dot(kv[1, :, span(b)], e.astype(BF16), preferred_element_type=F32)
            return top, total * fade + jnp.sum(fold(e, jnp.add), axis=0, keepdims=True), out

        top, total, out = lax.fori_loop(
            begin, end, forward, (jnp.full((1, wide), -1e30, F32), jnp.zeros((1, wide), F32), jnp.zeros((DH, wide), F32)))
        attended = (out / total).astype(BF16)
        oq[0, :, cols] = attended
        delta = jnp.sum(gt.astype(F32) * attended.astype(F32), axis=0, keepdims=True)
        share = 1.0 / total
        tail, left = jnp.zeros((spare, wide), F32), -delta
        for n in range(3):
            piece = left.astype(BF16).astype(F32)
            tail = jnp.where(line(wide) == n, piece, tail)
            left = left - piece
        gt = jnp.concatenate([gt, tail.astype(BF16)], axis=0)

        def backward(b, dq):
            w = score[span(b), :] * (share * jnp.exp2((peak[pl.ds(b, 1), :] - top) * power))
            ds = (w * jnp.dot(value[span(b), :], gt, preferred_element_type=F32)).astype(BF16)
            dkey[span(b), :] += jnp.dot(ds, q, preferred_element_type=F32)
            dvalue[span(b), :] += jnp.dot(w.astype(BF16), g, preferred_element_type=F32)
            return dq + jnp.dot(kv[0, :, span(b)], ds, preferred_element_type=F32)

        dq = lax.fori_loop(begin, end, backward, jnp.zeros((DH, wide), F32))
        oq[1, :, cols] = (dq * scale).astype(BF16)

    @pl.loop(0, total_rows // rows, unroll=8)
    def _(c):
        at = pl.ds(pl.multiple_of(c * rows, rows), rows)
        dkv[0, :, at] = (dkey[at, :] * scale).astype(BF16).T
        dkv[1, :, at] = dvalue[at, :].astype(BF16).T


def store_kernel(*refs):
    half = len(refs) // 2
    copies = [pltpu.make_async_copy(refs[n], refs[half + n], refs[-1].at[n]) for n in range(half)]
    for copy in copies:
        copy.start()
    for copy in copies:
        copy.wait()


def body(queries, keys, values, grad_out, frame_counts):
    T, H = lax.axis_size("tm"), lax.axis_size("head")
    R = T // HEADS
    rows = queries.shape[0]
    total_rows = rows * T * H
    mine = HEADS * rows
    kblock = 1024
    vmem = pl.BlockSpec(memory_space=pltpu.VMEM)
    hbm = pl.BlockSpec(memory_space=pltpu.HBM)
    place = pl.BlockSpec(memory_space=pl.ANY)
    smem = pl.BlockSpec(memory_space=pltpu.SMEM)
    dma = pltpu.SemaphoreType.DMA
    kv, qg = pl.pallas_call(
        functools.partial(gather_kernel, T, H, R),
        out_shape=(jax.ShapeDtypeStruct((2, DH, total_rows), BF16),
                   jax.ShapeDtypeStruct((2, DH, mine), BF16)),
        in_specs=[hbm] * 4,
        out_specs=(vmem, vmem),
        scratch_shapes=[
            pltpu.VMEM((HEADS, 2, DH, rows), BF16), pltpu.VMEM((HEADS, 2, DH, rows), BF16),
            pltpu.VMEM((4, rows, HEADS * DH), BF16), dma((4,)),
            dma((T,)), dma((T,)), dma((T,)), dma((T,)), dma((T, H)), dma((T, H))],
        compiler_params=pltpu.CompilerParams(
            collective_id=0, has_side_effects=True, vmem_limit_bytes=24 << 20),
        name="gather",
    )(queries, keys, values, grad_out)
    oq, dkv = pl.pallas_call(
        functools.partial(attention_kernel, T, H, R, kblock),
        out_shape=(jax.ShapeDtypeStruct((2, DH, mine), BF16),
                   jax.ShapeDtypeStruct((2, DH, total_rows), BF16)),
        in_specs=[smem, vmem, vmem],
        out_specs=(vmem, vmem),
        scratch_shapes=[
            pltpu.VMEM((total_rows, LANES), BF16), pltpu.VMEM((total_rows, LANES), BF16),
            pltpu.VMEM((total_rows, 2 * rows), F32),
            pltpu.VMEM((total_rows // kblock, 2 * rows), F32),
            pltpu.VMEM((total_rows, DH), F32), pltpu.VMEM((total_rows, DH), F32),
        ],
        compiler_params=pltpu.CompilerParams(vmem_limit_bytes=min(60 << 20, (8 << 20) + total_rows * 3584)),
        name="attention",
    )(frame_counts, kv, qg)
    block = jax.ShapeDtypeStruct((rows, HEADS * DH), BF16)
    outs = pl.pallas_call(
        functools.partial(scatter_kernel, T, H, R),
        out_shape=(block,) * 4,
        in_specs=[place, place],
        out_specs=(vmem,) * 4,
        scratch_shapes=[
            pltpu.VMEM((H - 1, T, 2, DH, rows), BF16),
            pltpu.VMEM((T, 2, DH, rows), BF16), pltpu.VMEM((T, 2, DH, rows), BF16),
            pltpu.VMEM((HEADS, 2, DH, rows), BF16), pltpu.VMEM((T, 2, DH, rows), BF16),
            dma((T + 1,)), dma((T, H)), dma((T, H)), dma((T,)), dma((T,)), dma((T,)), dma((T,))],
        compiler_params=pltpu.CompilerParams(
            collective_id=1, has_side_effects=True, vmem_limit_bytes=24 << 20),
        name="scatter",
    )(oq, dkv)
    return pl.pallas_call(
        store_kernel,
        out_shape=(block,) * 4,
        in_specs=[place] * 4,
        out_specs=(hbm,) * 4,
        scratch_shapes=[dma((4,))],
        name="store",
    )(*outs)


def solution(mesh):
    split = P(("tm", "head"), None)
    return jax.shard_map(
        body, mesh=mesh, in_specs=(split,) * 4 + (P(),), out_specs=(split,) * 4, check_vma=False)
```

```python
import functools
import math

import jax
import jax.numpy as jnp
from jax import lax
from jax.experimental import pallas as pl
from jax.experimental.pallas import tpu as pltpu
from jax.sharding import PartitionSpec as P

HEADS = 8
DH = 96
LANES = 128
MESH = pl.DeviceIdType.MESH
F32 = jnp.float32
BF16 = jnp.bfloat16


def greet(t, hd, T, H):
    barrier = pltpu.get_barrier_semaphore()
    for i in range(1, T):
        pl.semaphore_signal(barrier, inc=1, device_id=(lax.rem(t + i, T), hd), device_id_type=MESH)
    for j in range(1, H):
        pl.semaphore_signal(barrier, inc=1, device_id=(t, lax.rem(hd + j, H)), device_id_type=MESH)
    return barrier


def lanes(chunk, rows):
    return pl.ds(pl.multiple_of(chunk * rows, rows), rows)


def gather_kernel(T, H, R, q_ref, k_ref, v_ref, g_ref, kv, qg, kvs, qgs, held,
                  ls, zs, zr, qs, qr, ps, pr):
    rows = q_ref.shape[0]
    loads = [pltpu.make_async_copy(ref, held.at[n], ls.at[n])
             for n, ref in enumerate((k_ref, v_ref, q_ref, g_ref))]
    for load in loads:
        load.start()
    t, hd = lax.axis_index("tm"), lax.axis_index("head")
    barrier = greet(t, hd, T, H)

    def turn(dst, first):
        for n in range(2):
            loads[first + n].wait()
            flat = held[first + n].T
            for h in range(HEADS):
                dst[h, n] = flat[h * DH:(h + 1) * DH, :]

    turn(kvs, 0)
    pl.semaphore_wait(barrier, T + H - 2)

    def kv_copy(i, dest, owner):
        return pltpu.make_async_remote_copy(
            src_ref=kvs.at[lax.div(dest, R)], dst_ref=kv.at[:, :, lanes(owner * H + hd, rows)],
            send_sem=zs.at[i], recv_sem=zr.at[i], device_id=(dest, hd), device_id_type=MESH)

    def qg_copy(i, dest, owner):
        return pltpu.make_async_remote_copy(
            src_ref=qgs.at[lax.div(dest, R)], dst_ref=qg.at[:, :, lanes(lax.div(owner, R), rows)],
            send_sem=qs.at[i], recv_sem=qr.at[i], device_id=(dest, hd), device_id_type=MESH)

    def plane_copy(i, j, source, column):
        where = kv.at[:, :, lanes(source * H + column, rows)]
        return pltpu.make_async_remote_copy(
            src_ref=where, dst_ref=where, send_sem=ps.at[i, j], recv_sem=pr.at[i, j],
            device_id=(t, lax.rem(hd + j, H)), device_id_type=MESH)

    for i in range(1, T):
        kv_copy(i, lax.rem(t + i, T), t).start()
    kv[:, :, lanes(t * H + hd, rows)] = kvs[lax.div(t, R)]
    for j in range(1, H):
        plane_copy(0, j, t, hd).start()
    turn(qgs, 2)
    for i in range(R, T, R):
        qg_copy(i, lax.rem(t + i, T), t).start()
    qg[:, :, lanes(lax.div(t, R), rows)] = qgs[lax.div(t, R)]
    for i in range(1, T):
        source = lax.rem(t + T - i, T)
        kv_copy(i, lax.rem(t + i, T), source).wait_recv()
        for j in range(1, H):
            plane_copy(i, j, source, hd).start()
    for i in range(T):
        source = lax.rem(t + T - i, T)
        for j in range(1, H):
            plane_copy(i, j, source, hd).wait_send()
            plane_copy(i, j, source, lax.rem(hd + H - j, H)).wait_recv()
        if i:
            kv_copy(i, lax.rem(t + i, T), t).wait_send()
        if i and i % R == 0:
            qg_copy(i, lax.rem(t + i, T), source).wait()


def scatter_kernel(T, H, R, oq, dkv, att, gq, gk, gv, part, own, summed, home_o, home_k,
                   ls, ps, pr, os_, or_, ks, kr):
    rows = att.shape[0]
    t, hd = lax.axis_index("tm"), lax.axis_index("head")
    barrier = greet(t, hd, T, H)

    def own_load(i):
        target = lax.rem(t + i, T)
        return pltpu.make_async_copy(
            dkv.at[:, :, lanes(target * H + hd, rows)], own.at[target], ls.at[i])

    own_out = pltpu.make_async_copy(
        oq.at[:, :, lanes(lax.div(t, R), rows)], home_o.at[lax.div(t, R)], ls.at[T])
    for i in range(T):
        own_load(i).start()
    own_out.start()
    pl.semaphore_wait(barrier, T + H - 2)

    def plane_copy(i, j, target, column):
        return pltpu.make_async_remote_copy(
            src_ref=dkv.at[:, :, lanes(target * H + column, rows)], dst_ref=part.at[j - 1, target],
            send_sem=ps.at[i, j], recv_sem=pr.at[i, j], device_id=(t, column), device_id_type=MESH)

    def o_copy(i, dest, owner):
        return pltpu.make_async_remote_copy(
            src_ref=oq.at[:, :, lanes(lax.div(dest, R), rows)], dst_ref=home_o.at[lax.div(owner, R)],
            send_sem=os_.at[i], recv_sem=or_.at[i], device_id=(dest, hd), device_id_type=MESH)

    def k_copy(i, dest, owner):
        return pltpu.make_async_remote_copy(
            src_ref=summed.at[dest], dst_ref=home_k.at[owner],
            send_sem=ks.at[i], recv_sem=kr.at[i], device_id=(dest, hd), device_id_type=MESH)

    order = list(range(1, T)) + [0]
    for i in order:
        for j in range(1, H):
            plane_copy(i, j, lax.rem(t + i, T), lax.rem(hd + j, H)).start()
    for i in range(R, T, R):
        o_copy(i, lax.rem(t + i, T), t).start()
    for i in order:
        target = lax.rem(t + i, T)
        own_load(i).wait()
        total = own[target].astype(F32)
        for j in range(1, H):
            plane_copy(i, j, target, lax.rem(hd + j, H)).wait_recv()
            total = total + part[j - 1, target].astype(F32)
        if i:
            summed[target] = total.astype(BF16)
            k_copy(i, target, t).start()
        else:
            home_k[t] = total.astype(BF16)
    for i in range(R, T, R):
        o_copy(i, lax.rem(t + i, T), lax.rem(t + T - i, T)).wait()
    own_out.wait()
    att[...] = home_o[:, 0].reshape(HEADS * DH, rows).T
    gq[...] = home_o[:, 1].reshape(HEADS * DH, rows).T
    for i in order:
        target = lax.rem(t + i, T)
        for j in range(1, H):
            plane_copy(i, j, target, lax.rem(hd + j, H)).wait_send()
        if i:
            k_copy(i, target, lax.rem(t + T - i, T)).wait()
    for n, out in enumerate((gk, gv)):
        terms = home_k[:, n]
        if R > 1:
            terms = jnp.sum(terms.reshape(HEADS, R, DH, rows).astype(F32), axis=1).astype(BF16)
        out[...] = terms.reshape(HEADS * DH, rows).T


def attention_kernel(T, H, R, kblock, counts, kv, qg, oq, dkv, key, value, score, peak, dkey, dvalue):
    total_rows = kv.shape[2]
    rows = total_rows // (T * H)
    wide = 2 * rows
    pairs = qg.shape[2] // wide
    spare = key.shape[1] - DH
    scale = 1.0 / math.sqrt(DH)
    power = scale * math.log2(math.e)
    dkey[...] = jnp.zeros_like(dkey)
    dvalue[...] = jnp.zeros_like(dvalue)
    t, hd = lax.axis_index("tm"), lax.axis_index("head")
    bounds = []
    edge = 0
    for n in range(counts.shape[0] - 1):
        edge = edge + counts[n]
        bounds.append(edge)

    def first(frame):
        low = jnp.int32(0)
        for bound in bounds:
            low = jnp.where(frame >= bound, bound, low)
        return low

    def last(frame):
        high = jnp.int32(total_rows)
        for bound in bounds[::-1]:
            high = jnp.where(frame < bound, bound, high)
        return high

    def utterance(frame):
        index = jnp.zeros_like(frame)
        for bound in bounds:
            index = index + (frame >= bound).astype(jnp.int32)
        return index

    def line(n):
        return lax.broadcasted_iota(jnp.int32, (spare, n), 0)

    @pl.loop(0, total_rows // rows, unroll=8)
    def _(c):
        at = pl.ds(pl.multiple_of(c * rows, rows), rows)
        frame = c * rows + lax.broadcasted_iota(jnp.int32, (1, rows), 1)
        member = jnp.where(line(rows) == utterance(frame), 1.0, 0.0).astype(BF16)
        ones = jnp.where(line(rows) < 3, 1.0, 0.0).astype(BF16)
        key[at, :] = jnp.concatenate([kv[0, :, at], member], axis=0).T
        value[at, :] = jnp.concatenate([kv[1, :, at], ones], axis=0).T

    @pl.loop(0, pairs)
    def _(p):
        cols = pl.ds(pl.multiple_of(p * wide, wide), wide)
        qt, gt = qg[0, :, cols], qg[1, :, cols]
        q, g = qt.T, gt.T
        base0 = ((2 * p * R + lax.rem(t, R)) * H + hd) * rows
        base1 = (((2 * p + 1) * R + lax.rem(t, R)) * H + hd) * rows
        lane = lax.broadcasted_iota(jnp.int32, (1, wide), 1)
        frame = jnp.where(lane < rows, base0 + lane, base1 + lane - rows)
        hidden = (line(wide) != utterance(frame)) & (line(wide) < counts.shape[0])
        qt = jnp.concatenate([qt, jnp.where(hidden, -1e30, 0.0).astype(BF16)], axis=0)
        begin = lax.div(first(base0), kblock)
        end = lax.div(last(base1 + rows - 1) + kblock - 1, kblock)

        def span(b):
            return pl.ds(pl.multiple_of(b * kblock, kblock), kblock)

        def fold(x, op):
            parts = [x[n * 64:(n + 1) * 64] for n in range(kblock // 64)]
            while len(parts) > 1:
                parts = [op(parts[2 * n], parts[2 * n + 1]) for n in range(len(parts) // 2)]
            return parts[0]

        def forward(b, carry):
            reach, total, out = carry
            s = jnp.dot(key[span(b), :], qt, preferred_element_type=F32)
            top = jnp.maximum(reach, jnp.max(fold(s, jnp.maximum), axis=0, keepdims=True))
            e = jnp.exp2((s - top) * power)
            fade = jnp.exp2((reach - top) * power)
            score[span(b), :] = e
            peak[pl.ds(b, 1), :] = top
            out = out * fade + jnp.dot(kv[1, :, span(b)], e.astype(BF16), preferred_element_type=F32)
            return top, total * fade + jnp.sum(fold(e, jnp.add), axis=0, keepdims=True), out

        top, total, out = lax.fori_loop(
            begin, end, forward, (jnp.full((1, wide), -1e30, F32), jnp.zeros((1, wide), F32), jnp.zeros((DH, wide), F32)))
        attended = (out / total).astype(BF16)
        oq[0, :, cols] = attended
        delta = jnp.sum(gt.astype(F32) * attended.astype(F32), axis=0, keepdims=True)
        share = 1.0 / total
        tail, left = jnp.zeros((spare, wide), F32), -delta
        for n in range(3):
            piece = left.astype(BF16).astype(F32)
            tail = jnp.where(line(wide) == n, piece, tail)
            left = left - piece
        gt = jnp.concatenate([gt, tail.astype(BF16)], axis=0)

        def backward(b, dq):
            w = score[span(b), :] * (share * jnp.exp2((peak[pl.ds(b, 1), :] - top) * power))
            ds = (w * jnp.dot(value[span(b), :], gt, preferred_element_type=F32)).astype(BF16)
            dkey[span(b), :] += jnp.dot(ds, q, preferred_element_type=F32)
            dvalue[span(b), :] += jnp.dot(w.astype(BF16), g, preferred_element_type=F32)
            return dq + jnp.dot(kv[0, :, span(b)], ds, preferred_element_type=F32)

        dq = lax.fori_loop(begin, end, backward, jnp.zeros((DH, wide), F32))
        oq[1, :, cols] = (dq * scale).astype(BF16)

    @pl.loop(0, total_rows // rows, unroll=8)
    def _(c):
        at = pl.ds(pl.multiple_of(c * rows, rows), rows)
        dkv[0, :, at] = (dkey[at, :] * scale).astype(BF16).T
        dkv[1, :, at] = dvalue[at, :].astype(BF16).T


def store_kernel(*refs):
    half = len(refs) // 2
    copies = [pltpu.make_async_copy(refs[n], refs[half + n], refs[-1].at[n]) for n in range(half)]
    for copy in copies:
        copy.start()
    for copy in copies:
        copy.wait()


def body(queries, keys, values, grad_out, frame_counts):
    T, H = lax.axis_size("tm"), lax.axis_size("head")
    R = T // HEADS
    rows = queries.shape[0]
    total_rows = rows * T * H
    mine = HEADS * rows
    kblock = 1024
    vmem = pl.BlockSpec(memory_space=pltpu.VMEM)
    hbm = pl.BlockSpec(memory_space=pltpu.HBM)
    place = pl.BlockSpec(memory_space=pl.ANY)
    smem = pl.BlockSpec(memory_space=pltpu.SMEM)
    dma = pltpu.SemaphoreType.DMA
    kv, qg = pl.pallas_call(
        functools.partial(gather_kernel, T, H, R),
        out_shape=(jax.ShapeDtypeStruct((2, DH, total_rows), BF16),
                   jax.ShapeDtypeStruct((2, DH, mine), BF16)),
        in_specs=[hbm] * 4,
        out_specs=(vmem, vmem),
        scratch_shapes=[
            pltpu.VMEM((HEADS, 2, DH, rows), BF16), pltpu.VMEM((HEADS, 2, DH, rows), BF16),
            pltpu.VMEM((4, rows, HEADS * DH), BF16), dma((4,)),
            dma((T,)), dma((T,)), dma((T,)), dma((T,)), dma((T, H)), dma((T, H))],
        compiler_params=pltpu.CompilerParams(
            collective_id=0, has_side_effects=True, vmem_limit_bytes=24 << 20),
        name="gather",
    )(queries, keys, values, grad_out)
    oq, dkv = pl.pallas_call(
        functools.partial(attention_kernel, T, H, R, kblock),
        out_shape=(jax.ShapeDtypeStruct((2, DH, mine), BF16),
                   jax.ShapeDtypeStruct((2, DH, total_rows), BF16)),
        in_specs=[smem, vmem, vmem],
        out_specs=(vmem, vmem),
        scratch_shapes=[
            pltpu.VMEM((total_rows, LANES), BF16), pltpu.VMEM((total_rows, LANES), BF16),
            pltpu.VMEM((total_rows, 2 * rows), F32),
            pltpu.VMEM((total_rows // kblock, 2 * rows), F32),
            pltpu.VMEM((total_rows, DH), F32), pltpu.VMEM((total_rows, DH), F32),
        ],
        compiler_params=pltpu.CompilerParams(vmem_limit_bytes=min(60 << 20, (8 << 20) + total_rows * 3584)),
        name="attention",
    )(frame_counts, kv, qg)
    block = jax.ShapeDtypeStruct((rows, HEADS * DH), BF16)
    outs = pl.pallas_call(
        functools.partial(scatter_kernel, T, H, R),
        out_shape=(block,) * 4,
        in_specs=[place, place],
        out_specs=(vmem,) * 4,
        scratch_shapes=[
            pltpu.VMEM((H - 1, T, 2, DH, rows), BF16),
            pltpu.VMEM((T, 2, DH, rows), BF16), pltpu.VMEM((T, 2, DH, rows), BF16),
            pltpu.VMEM((HEADS, 2, DH, rows), BF16), pltpu.VMEM((T, 2, DH, rows), BF16),
            dma((T + 1,)), dma((T, H)), dma((T, H)), dma((T,)), dma((T,)), dma((T,)), dma((T,))],
        compiler_params=pltpu.CompilerParams(
            collective_id=1, has_side_effects=True, vmem_limit_bytes=24 << 20),
        name="scatter",
    )(oq, dkv)
    return pl.pallas_call(
        store_kernel,
        out_shape=(block,) * 4,
        in_specs=[vmem] * 4,
        out_specs=(hbm,) * 4,
        scratch_shapes=[dma((4,))],
        compiler_params=pltpu.CompilerParams(vmem_limit_bytes=8 << 20),
        name="store",
    )(*outs)


def solution(mesh):
    split = P(("tm", "head"), None)
    return jax.shard_map(
        body, mesh=mesh, in_specs=(split,) * 4 + (P(),), out_specs=(split,) * 4, check_vma=False)
```
